32 devices in a mesh: dp: 16 (over z, y, x), mp: 2 (over core).
Axes of the slice: x: 2, y: 2, z: 4, core: 2. Of those that a mesh axis runs over, the one named last changes fastest.
Arguments:
- layer_input: bfloat16 [8192, 768], P(('dp', 'mp')), may hold values from -6 to 6
- upstream_grad: bfloat16 [8192, 768], P(('dp', 'mp')), may hold values from -6 to 6
- doc_lengths: int32 [16, 4], P('dp'), may hold values from 1 to 509, as said below
- qkv_weight: float32 [3, 768, 768], P(None, ('mp', 'dp')), may hold values from -0.21875 to 0.21875
- out_weight: float32 [768, 768], P(('mp', 'dp')), may hold values from -0.875 to 0.875
- gate_weight: float32 [3072, 768], P(('mp', 'dp')), may hold values from -0.21875 to 0.21875
- up_weight: float32 [3072, 768], P(('mp', 'dp')), may hold values from -0.21875 to 0.21875
- down_weight: float32 [3072, 768], P(('mp', 'dp')), may hold values from -0.109375 to 0.109375
- qkv_momentum: float32 [3, 768, 768], P(None, ('mp', 'dp')), may hold values from -271.529 to 271.529
- out_momentum: float32 [768, 768], P(('mp', 'dp')), may hold values from -271.529 to 271.529
- gate_momentum: float32 [3072, 768], P(('mp', 'dp')), may hold values from -271.529 to 271.529
- up_momentum: float32 [3072, 768], P(('mp', 'dp')), may hold values from -271.529 to 271.529
- down_momentum: float32 [3072, 768], P(('mp', 'dp')), may hold values from -271.529 to 271.529
- norm_gains: float32 [2, 768], P(None, 'dp'), may hold values from 0.5 to 1.5
- norm_biases: float32 [2, 768], P(None, 'dp'), may hold values from -3 to 3
- adam_first: float32 [4, 768], P(None, 'dp'), may hold values from -56 to 56
- adam_second: float32 [4, 768], P(None, 'dp'), may hold values from 245.76 to 983.04
Outputs:
- mixed: bfloat16 [8192, 768], P(('dp', 'mp'))
- input_grad: float32 [8192, 768], P(('dp', 'mp'))
- qkv_updated: float32 [3, 768, 768], P(None, ('mp', 'dp'))
- out_updated: float32 [768, 768], P(('mp', 'dp'))
- gate_updated: float32 [3072, 768], P(('mp', 'dp'))
- up_updated: float32 [3072, 768], P(('mp', 'dp'))
- down_updated: float32 [3072, 768], P(('mp', 'dp'))
- qkv_carried: float32 [3, 768, 768], P(None, ('mp', 'dp'))
- out_carried: float32 [768, 768], P(('mp', 'dp'))
- gate_carried: float32 [3072, 768], P(('mp', 'dp'))
- up_carried: float32 [3072, 768], P(('mp', 'dp'))
- down_carried: float32 [3072, 768], P(('mp', 'dp'))
- norm_updated: float32 [4, 768], P(None, 'dp')
- norm_first: float32 [4, 768], P(None, 'dp')
- norm_second: float32 [4, 768], P(None, 'dp')
The draws below stay inside these ranges and needn't reach their ends.
Inputs may be any that keep to these rules, and one draw needn't show every extreme that they name: `doc_lengths`: row p lists the lengths of the 4 documents packed from the first slot of packed sequence p; a row sums to at most 512, the last row to exactly 512 with its first document 512 - 3 long; the remaining slots are padding.
All inputs are finite; a program needn't handle non-finite values.
Results may differ from the reference program's by a relative error of at most 0.035.
Values may be sent and summed in bfloat16 or wider, within the bound.
No kernel may reach another device: no remote copies, remote signals or barrier semaphores. Data moves between devices by JAX's collectives and lax.ppermute only.
A program may use at most 192 MiB of HBM per device.

```python
import math
import jax
import jax.numpy as jnp
from jax import lax

D = 768
H = 12
HD = 64
FF = 3072
TOK_DEV = 512
DOCS = 4
ORTHO_STEPS = 5
STEP_COUNT = 10
PACKS = 16
TOKENS = 8192


def ramp_rows(noise, lowest, row_axis):
    count_rows = noise.shape[row_axis]
    ramp = lowest + jnp.arange(count_rows, dtype=jnp.float32) / max(count_rows - 1, 1)
    expand = [1] * noise.ndim
    expand[row_axis] = count_rows
    return noise * ramp.reshape(expand) * (0.5 * (TOK_DEV * PACKS) ** 0.5)


def draw_doc_lengths(key, part):
    key = jax.random.fold_in(key, 5)
    first_key, second_key, third_key = jax.random.split(key, 3)
    pack_ids = jnp.arange(PACKS, dtype=jnp.int32)
    span_packs = max(PACKS - 1, 1)
    ramped = TOK_DEV * (span_packs + 2 * pack_ids) // (3 * span_packs)
    jitter = jax.random.randint(first_key, (PACKS,), 0, TOK_DEV // 16 + 1, dtype=jnp.int32)
    totals = jnp.where(pack_ids == PACKS - 1, TOK_DEV, ramped - jitter).astype(jnp.int32)
    exponent = jax.random.randint(second_key, (PACKS, DOCS), 2, 12, dtype=jnp.int32)
    random_bits = jax.random.randint(third_key, (PACKS, DOCS), 0, 1 << 20, dtype=jnp.int32)
    raw_sizes = 1 + jnp.remainder(random_bits, jnp.left_shift(jnp.ones_like(exponent), exponent))
    spare_rows = totals - DOCS
    shares = raw_sizes * spare_rows[:, None] // jnp.sum(raw_sizes, axis=1, keepdims=True).astype(jnp.int32)
    lengths = (1 + shares).astype(jnp.int32)
    shortfall = totals - jnp.sum(lengths, axis=1).astype(jnp.int32)
    column_ids = jnp.arange(DOCS, dtype=jnp.int32)[None, :]
    lengths = (lengths + jnp.where(column_ids == 0, shortfall[:, None], 0)).astype(jnp.int32)
    last_row = jnp.where(column_ids[0] == 0, TOK_DEV - DOCS + 1, 1).astype(jnp.int32)
    return jnp.where(pack_ids[:, None] == PACKS - 1, last_row[None, :], lengths).astype(jnp.int32)


def draw_qkv_momentum(key, part):
    key = jax.random.fold_in(key, 11)
    return ramp_rows(jnp.clip(jax.random.normal(key, (3, D, D), jnp.float32), -4.0, 4.0), 0.5, 1)


def draw_out_momentum(key, part):
    key = jax.random.fold_in(key, 13)
    return ramp_rows(jnp.clip(jax.random.normal(key, (D, D), jnp.float32), -4.0, 4.0), 0.5, 0)


def draw_gate_momentum(key, part):
    key = jax.random.fold_in(key, 17)
    return ramp_rows(jnp.clip(jax.random.normal(key, (FF, D), jnp.float32), -4.0, 4.0), 0.5, 0)


def draw_up_momentum(key, part):
    key = jax.random.fold_in(key, 19)
    return ramp_rows(jnp.clip(jax.random.normal(key, (FF, D), jnp.float32), -4.0, 4.0), 0.5, 0)


def draw_down_momentum(key, part):
    key = jax.random.fold_in(key, 23)
    return ramp_rows(jnp.clip(jax.random.normal(key, (FF, D), jnp.float32), -4.0, 4.0), 0.5, 0)


def levels(own_key, shape, shards, least, top_value):
    def one(dim, blocks):
        steps = jax.random.uniform(jax.random.fold_in(jax.random.fold_in(own_key, 6), dim), (blocks,), jnp.float32, least / len(shards), top_value / len(shards))
        return jnp.repeat(jnp.exp(steps), shape[dim] // blocks).reshape((-1,) + (1,) * (len(shape) - dim - 1))

    level = one(*shards[0])
    for cut in shards[1:]:
        level = level * one(*cut)
    return level


def bell_draw(key, dims, width, most, cuts=(), kind=jnp.bfloat16):
    level = levels(key, dims, cuts, -0.22, 0.18) if cuts else 1.0
    array = jax.random.normal(key, dims, jnp.float32) * width * level
    return jnp.minimum(jnp.maximum(array, -most), most).astype(kind)


def setup_inputs(seed: int = 0) -> dict:
    key_of = jax.random.split(jax.random.key(seed), 18)
    return {
        "layer_input": bell_draw(key_of[0], (TOKENS, D), 1.0, 6.0, ((0, 32),)),
        "upstream_grad": bell_draw(key_of[1], (TOKENS, D), 1.0, 6.0, ((0, 32),)),
        "doc_lengths": draw_doc_lengths(jax.random.fold_in(key_of[17], 71), 0),
        "qkv_weight": bell_draw(key_of[3], (3, D, D), D ** -0.5, 0.21875, ((1, 32),), jnp.float32),
        "out_weight": bell_draw(key_of[4], (D, D), (D // 16) ** -0.5, 0.875, ((0, 32),), jnp.float32),
        "gate_weight": bell_draw(key_of[5], (FF, D), D ** -0.5, 0.21875, ((0, 32),), jnp.float32),
        "up_weight": bell_draw(key_of[6], (FF, D), D ** -0.5, 0.21875, ((0, 32),), jnp.float32),
        "down_weight": bell_draw(key_of[7], (FF, D), FF ** -0.5, 0.109375, ((0, 32),), jnp.float32),
        "qkv_momentum": draw_qkv_momentum(jax.random.fold_in(key_of[17], 71), 0),
        "out_momentum": draw_out_momentum(jax.random.fold_in(key_of[17], 71), 0),
        "gate_momentum": draw_gate_momentum(jax.random.fold_in(key_of[17], 71), 0),
        "up_momentum": draw_up_momentum(jax.random.fold_in(key_of[17], 71), 0),
        "down_momentum": draw_down_momentum(jax.random.fold_in(key_of[17], 71), 0),
        "norm_gains": jnp.clip(1.0 + 0.1 * jax.random.normal(key_of[13], (2, D), jnp.float32), 0.5, 1.5),
        "norm_biases": bell_draw(key_of[14], (2, D), 0.3, 3.0, ((1, 16),), jnp.float32),
        "adam_first": bell_draw(key_of[15], (4, D), (0.1 * (TOK_DEV * PACKS) ** 0.5), 56.0, ((1, 16),), jnp.float32),
        "adam_second": jnp.clip(jnp.exp(math.log(983.04) - 1.3862944 * jax.random.uniform(key_of[16], (4, D), jnp.float32) ** levels(key_of[16], (4, D), ((1, 16),), -0.2, 0.2)), 245.76, 983.04),
    }


NORM_EPSILON = 1e-12
ROPE_BASE = 1000.0
SCHULZ_LINEAR = 3.4445
SCHULZ_CUBIC = -4.775
SCHULZ_QUINTIC = 2.0315
MOMENTUM_KEEP = 0.5
ORTHO_RATE = 0.2
WEIGHT_DECAY = 0.01
ADAM_RATE = 0.2
BETA_FIRST = 0.9
BETA_SECOND = 0.95
ADAM_EPSILON = 1e-08

@jax.custom_vjp
def low(v):
    return lax.optimization_barrier(v.astype(jnp.bfloat16)).astype(jnp.float32)

@jax.custom_vjp
def low_back(v):
    return v

def low_keep(v):
    return (low(v), None)

def low_pass(kept, grad):
    return (grad,)

def back_keep(v):
    return (v, None)

def back_low(kept, grad):
    return (low(grad),)
low.defvjp(low_keep, low_pass)
low_back.defvjp(back_keep, back_low)

def rounded(value):
    return lax.optimization_barrier(value.astype(jnp.bfloat16)).astype(jnp.float32)

def document_layout(lengths, total_rows):
    ends = jnp.cumsum(lengths).astype(jnp.int32)
    starts = (ends - lengths).astype(jnp.int32)
    row_ids = jnp.arange(total_rows, dtype=jnp.int32)
    segments = lax.optimization_barrier(jnp.sum((row_ids[:, None] >= ends[None, :]).astype(jnp.int32), axis=1)).astype(jnp.int32)
    used_rows = ends[-1]
    matches = segments[:, None] == jnp.arange(lengths.shape[0], dtype=jnp.int32)[None, :]
    anchor = lax.optimization_barrier(jnp.sum(jnp.where(matches, starts[None, :], 0), axis=1)).astype(jnp.int32)
    anchor = anchor + jnp.where(segments == lengths.shape[0], used_rows, 0).astype(jnp.int32)
    positions = row_ids - anchor
    validity = (row_ids < used_rows).astype(jnp.float32)
    return (segments, positions, validity)

def rotary_tables(positions):
    half_width = HD // 2
    exponents = jnp.arange(half_width, dtype=jnp.float32) * (2.0 / HD)
    frequency = jnp.power(jnp.float32(ROPE_BASE), -exponents)
    angles = positions.astype(jnp.float32)[:, None] * frequency[None, :]
    return (jnp.cos(angles), jnp.sin(angles))

def rotate(vectors, cosine_table, sine_table):
    half_width = vectors.shape[-1] // 2
    leading = vectors[..., :half_width]
    trailing = vectors[..., half_width:]
    cosine_part = cosine_table[:, None, :]
    sine_part = sine_table[:, None, :]
    return jnp.concatenate([leading * cosine_part - trailing * sine_part, trailing * cosine_part + leading * sine_part], axis=-1)

def layer_norm(values, gain, bias):
    centered = values - lax.optimization_barrier(jnp.mean(values, axis=-1, keepdims=True))
    inverse = lax.rsqrt(lax.optimization_barrier(jnp.mean(centered * centered, axis=-1, keepdims=True)) + NORM_EPSILON)
    return centered * inverse * gain + bias

def attention(queries, key_vectors, value_vectors, segments):
    total_rows = queries.shape[0]
    block_rows = min(512, total_rows)
    score_scale = HD ** (-0.5)

    def one_block(block_index):
        offset = (block_index * block_rows).astype(jnp.int32)
        query_rows = lax.dynamic_slice_in_dim(queries, offset, block_rows, 0)
        query_segments = lax.dynamic_slice_in_dim(segments, offset, block_rows, 0)
        scores = jnp.einsum('qhd,khd->hqk', query_rows, key_vectors, precision=lax.Precision.HIGHEST)
        scores = low_back(scores * score_scale)
        allowed = (query_segments[:, None] == segments[None, :])[None]
        scores = jnp.where(allowed, scores, -1e+30)
        peak = lax.optimization_barrier(jnp.max(scores, axis=-1, keepdims=True))
        expanded = jnp.where(allowed, jnp.exp(scores - peak), 0.0)
        weights = low(expanded / lax.optimization_barrier(jnp.sum(expanded, axis=-1, keepdims=True)))
        return jnp.einsum('hqk,khd->qhd', weights, value_vectors, precision=lax.Precision.HIGHEST)
    blocks = lax.map(jax.checkpoint(one_block), jnp.arange(total_rows // block_rows, dtype=jnp.int32))
    return blocks.reshape(queries.shape)

def block_forward(tokens, params, segments, positions):
    qkv_weight, out_weight, gate_weight, up_weight, down_weight, norm_gains, norm_biases = params
    gains = low(norm_gains)
    biases = low(norm_biases)
    total_rows = tokens.shape[0]
    highest = lax.Precision.HIGHEST
    projected = low_back(jnp.dot(tokens, low(qkv_weight).reshape(3 * D, D).T, precision=highest))
    columns_split = projected.reshape(total_rows, 3, H, HD)
    cosine_table, sine_table = rotary_tables(positions)
    queries = low(rotate(columns_split[:, 0], cosine_table, sine_table))
    key_vectors = low(rotate(columns_split[:, 1], cosine_table, sine_table))
    value_vectors = low(columns_split[:, 2])
    attended = attention(queries, key_vectors, value_vectors, segments).reshape(total_rows, D)
    attended = low(low_back(attended))
    branch = low_back(jnp.dot(attended, low(out_weight), precision=highest))
    first_norm = layer_norm(tokens + branch, gains[0], biases[0])
    inner = low(first_norm)
    gate_pre = low_back(jnp.dot(inner, low(gate_weight).T, precision=highest))
    up_pre = low_back(jnp.dot(inner, low(up_weight).T, precision=highest))
    activated = low(gate_pre * jax.nn.sigmoid(gate_pre) * up_pre)
    feed = low_back(jnp.dot(activated, low(down_weight), precision=highest))
    return layer_norm(first_norm + feed, gains[1], biases[1])

def add_pair(left, right):
    return left + right

def orthogonalize(matrix):
    current = matrix.astype(jnp.bfloat16)
    total = jnp.sum(jnp.square(current.astype(jnp.float32)))
    current = (current.astype(jnp.float32) / (jnp.sqrt(total) + 1e-07)).astype(jnp.bfloat16)
    for repeat in range(ORTHO_STEPS):
        gram = jnp.dot(current.T, current, preferred_element_type=jnp.float32).astype(jnp.bfloat16)
        mixing = SCHULZ_CUBIC * gram.astype(jnp.float32) + SCHULZ_QUINTIC * jnp.dot(gram, gram, preferred_element_type=jnp.float32)
        current = (SCHULZ_LINEAR * current.astype(jnp.float32) + jnp.dot(current, mixing.astype(jnp.bfloat16), preferred_element_type=jnp.float32)).astype(jnp.bfloat16)
    return current.astype(jnp.float32)

def reference(layer_input, upstream_grad, doc_lengths, qkv_weight, out_weight, gate_weight, up_weight, down_weight, qkv_momentum, out_momentum, gate_momentum, up_momentum, down_momentum, norm_gains, norm_biases, adam_first, adam_second):
    params = (qkv_weight, out_weight, gate_weight, up_weight, down_weight, norm_gains, norm_biases)
    pack_tokens = layer_input.reshape(PACKS, TOK_DEV, D)
    pack_grads = upstream_grad.reshape(PACKS, TOK_DEV, D)

    def pack_step(totals, inputs):
        tokens, cotangent, lengths = inputs
        segments, positions, validity = document_layout(lengths, TOK_DEV)

        def forward(tokens_value, params_value):
            return block_forward(tokens_value, params_value, segments, positions)
        outputs, pullback = jax.vjp(forward, tokens.astype(jnp.float32), params)
        token_grad, param_grads = pullback(cotangent.astype(jnp.float32) * validity[:, None])
        totals = jax.tree.map(add_pair, totals, param_grads)
        return (totals, (outputs.astype(jnp.bfloat16), token_grad))
    zeros = jax.tree.map(jnp.zeros_like, params)
    grads, (mixed, input_grad) = lax.scan(pack_step, zeros, (pack_tokens, pack_grads, doc_lengths))
    mixed = mixed.reshape(TOKENS, D)
    input_grad = input_grad.reshape(TOKENS, D)
    weights = (qkv_weight, out_weight, gate_weight, up_weight, down_weight)
    momenta = (qkv_momentum, out_momentum, gate_momentum, up_momentum, down_momentum)
    row_totals = (3 * D, D, FF, FF, FF)
    updated = []
    carried_all = []
    for weight, moment, gradient, row_total in zip(weights, momenta, grads[:5], row_totals):
        carried = MOMENTUM_KEEP * moment + gradient
        ortho = orthogonalize(carried.reshape(row_total, D)).reshape(weight.shape)
        updated.append(weight * (1.0 - ORTHO_RATE * WEIGHT_DECAY) - ORTHO_RATE * 0.2 * math.sqrt(row_total) * ortho)
        carried_all.append(carried)
    norm_now = jnp.concatenate([norm_gains, norm_biases], axis=0)
    norm_grad = jnp.concatenate([grads[5], grads[6]], axis=0)
    norm_first = BETA_FIRST * adam_first + (1.0 - BETA_FIRST) * norm_grad
    norm_second = BETA_SECOND * adam_second + (1.0 - BETA_SECOND) * norm_grad * norm_grad
    first_hat = norm_first / (1.0 - BETA_FIRST ** STEP_COUNT)
    second_hat = norm_second / (1.0 - BETA_SECOND ** STEP_COUNT)
    norm_updated = norm_now - ADAM_RATE * first_hat / (jnp.sqrt(second_hat) + ADAM_EPSILON)
    return (mixed, input_grad, updated[0], updated[1], updated[2], updated[3], updated[4], carried_all[0], carried_all[1], carried_all[2], carried_all[3], carried_all[4], norm_updated, norm_first, norm_second)
```

```python
import math

import jax
import jax.numpy as jnp
from jax import lax
from jax.sharding import PartitionSpec as P

D = 768
HD = 64
FF = 3072
ORTHO_STEPS = 5
STEP_COUNT = 10


NORM_EPSILON = 1e-12
ROPE_BASE = 1000.0
SCHULZ_LINEAR = 3.4445
SCHULZ_CUBIC = -4.775
SCHULZ_QUINTIC = 2.0315
MOMENTUM_KEEP = 0.5
ORTHO_RATE = 0.2
WEIGHT_DECAY = 0.01
ADAM_RATE = 0.2
BETA_FIRST = 0.9
BETA_SECOND = 0.95
ADAM_EPSILON = 1e-08


def rotary_tables(positions):
    half_width = HD // 2
    exponents = jnp.arange(half_width, dtype=jnp.float32) * (2.0 / HD)
    frequency = jnp.power(jnp.float32(ROPE_BASE), -exponents)
    angles = positions.astype(jnp.float32)[:, None] * frequency[None, :]
    return (jnp.cos(angles), jnp.sin(angles))


def rotate(vectors, cosine_table, sine_table):
    half_width = vectors.shape[-1] // 2
    leading = vectors[..., :half_width]
    trailing = vectors[..., half_width:]
    cosine_part = cosine_table[:, None, :]
    sine_part = sine_table[:, None, :]
    return jnp.concatenate(
        [
            leading * cosine_part - trailing * sine_part,
            trailing * cosine_part + leading * sine_part,
        ],
        axis=-1,
    )


def unrotate(gradients, cosine_table, sine_table):
    half_width = gradients.shape[-1] // 2
    leading = gradients[..., :half_width]
    trailing = gradients[..., half_width:]
    cosine_part = cosine_table[:, None, :]
    sine_part = sine_table[:, None, :]
    return jnp.concatenate(
        [
            leading * cosine_part + trailing * sine_part,
            trailing * cosine_part - leading * sine_part,
        ],
        axis=-1,
    )


def layer_norm(values, gain, bias):
    centered = values - jnp.mean(values, axis=-1, keepdims=True)
    inverse = lax.rsqrt(jnp.mean(centered * centered, axis=-1, keepdims=True) + NORM_EPSILON)
    normed = centered * inverse
    return (normed * gain + bias, normed, inverse)


def norm_back(incoming, normed, inverse, gain):
    scaled = incoming * gain
    inner = (
        scaled
        - jnp.mean(scaled, axis=-1, keepdims=True)
        - normed * jnp.mean(scaled * normed, axis=-1, keepdims=True)
    )
    return (inner * inverse, jnp.sum(incoming * normed, axis=0), jnp.sum(incoming, axis=0))


def times_transposed(left, right):
    return lax.dot_general(
        left, right, (((1,), (1,)), ((), ())), preferred_element_type=jnp.float32
    )


def transposed_times(left, right):
    return lax.dot_general(
        left, right, (((0,), (0,)), ((), ())), preferred_element_type=jnp.float32
    )


def probabilities(query_rows, key_vectors, query_segments, segments):
    scores = jnp.einsum(
        "qhd,khd->hqk", query_rows, key_vectors, preferred_element_type=jnp.float32
    ) * HD ** (-0.5)
    allowed = (query_segments[:, None] == segments[None, :])[None]
    scores = jnp.where(allowed, scores, -1e30)
    peak = jnp.max(scores, axis=-1, keepdims=True)
    expanded = jnp.where(allowed, jnp.exp(scores - peak), 0.0)
    return expanded / jnp.sum(expanded, axis=-1, keepdims=True)


def attend(queries, key_vectors, value_vectors, segments):
    total_rows = queries.shape[0]
    block_rows = min(512, total_rows)

    def one_block(block_index):
        weights = probabilities(queries, key_vectors, segments, segments)
        return jnp.einsum(
            "hqk,khd->qhd",
            weights.astype(jnp.bfloat16),
            value_vectors,
            preferred_element_type=jnp.float32,
        )

    blocks = lax.map(one_block, jnp.arange(total_rows // block_rows, dtype=jnp.int32))
    return blocks.reshape(queries.shape)


def attend_back(queries, key_vectors, value_vectors, segments, heads_grad):
    total_rows = queries.shape[0]
    block_rows = min(512, total_rows)
    score_scale = HD ** (-0.5)

    def one_block(carry, block_index):
        key_grad, value_grad = carry
        weights = probabilities(queries, key_vectors, segments, segments)
        value_grad = value_grad + jnp.einsum(
            "hqk,qhd->khd",
            weights.astype(jnp.bfloat16),
            heads_grad,
            preferred_element_type=jnp.float32,
        )
        weight_grad = jnp.einsum(
            "qhd,khd->hqk", heads_grad, value_vectors, preferred_element_type=jnp.float32
        )
        centre = jnp.sum(weights * weight_grad, axis=-1, keepdims=True)
        score_grad = (weights * (weight_grad - centre)).astype(jnp.bfloat16)
        query_grad = (
            jnp.einsum("hqk,khd->qhd", score_grad, key_vectors, preferred_element_type=jnp.float32)
            * score_scale
        )
        key_grad = (
            key_grad
            + jnp.einsum("hqk,qhd->khd", score_grad, queries, preferred_element_type=jnp.float32)
            * score_scale
        )
        return ((key_grad, value_grad), query_grad)

    zeros = jnp.zeros(key_vectors.shape, jnp.float32)
    (key_grad, value_grad), query_blocks = lax.scan(
        one_block, (zeros, zeros), jnp.arange(total_rows // block_rows, dtype=jnp.int32)
    )
    return (query_blocks.reshape(queries.shape), key_grad, value_grad)


def swap(value):
    return lax.ppermute(value, "mp", [(0, 1), (1, 0)])


def flip(value, mask):
    count = lax.axis_size("dp")
    return lax.ppermute(value, "dp", [(i, i ^ mask) for i in range(count)])


def index_bits(count):
    bits = count.bit_length() - 1
    side = (bits - 2) // 2
    return (
        [1 << k for k in range(bits - 2, bits)],
        [1 << k for k in range(side)],
        [1 << k for k in range(side, bits - 2)],
    )


def block_codes(count):
    z_bits, x_bits, y_bits = index_bits(count)
    codes = [0]
    for mask in z_bits + x_bits + y_bits:
        codes = codes + [code ^ mask for code in codes]
    return codes


def lane_split(width):
    return width // 256 * 128


def gather_blocks(shard):
    z_bits, x_bits, y_bits = index_bits(lax.axis_size("dp"))
    low, high = z_bits
    shard = shard[None]
    column = jnp.concatenate(
        [shard, flip(shard, low), flip(shard, high), flip(shard, low ^ high)], axis=0
    )
    if len(x_bits) > 1:
        for mask in x_bits + y_bits:
            column = jnp.concatenate([column, flip(column, mask)], axis=0)
        return column
    x_mask, y_mask = x_bits[0], y_bits[0]
    cut = lane_split(column.shape[-1])
    along_x, along_y = flip(column, x_mask), flip(column, y_mask)
    across = jnp.concatenate(
        [flip(along_y[..., :cut], x_mask), flip(along_x[..., cut:], y_mask)], axis=-1
    )
    return jnp.concatenate([column, along_x, along_y, across], axis=0)


def scatter_blocks(blocks):
    z_bits, x_bits, y_bits = index_bits(lax.axis_size("dp"))

    def sent(value, mask):
        return flip(value.astype(jnp.bfloat16), mask).astype(jnp.float32)

    if len(x_bits) > 1:
        for mask in reversed(x_bits + y_bits):
            half = blocks.shape[0] // 2
            blocks = blocks[:half].astype(jnp.float32) + sent(blocks[half:], mask)
    else:
        x_mask, y_mask = x_bits[0], y_bits[0]
        cut = lane_split(blocks.shape[-1])
        here, along_x, along_y, across = [blocks[4 * k : 4 * k + 4] for k in range(4)]
        by_x = sent(across[..., :cut], x_mask)
        by_y = sent(across[..., cut:], y_mask)
        along_y = jnp.concatenate(
            [along_y[..., :cut].astype(jnp.float32) + by_x, along_y[..., cut:].astype(jnp.float32)],
            axis=-1,
        )
        along_x = jnp.concatenate(
            [along_x[..., :cut].astype(jnp.float32), along_x[..., cut:].astype(jnp.float32) + by_y],
            axis=-1,
        )
        blocks = here.astype(jnp.float32) + sent(along_x, x_mask) + sent(along_y, y_mask)
    low, high = z_bits
    return (
        blocks[0] + sent(blocks[1], low) + sent(blocks[2], high) + sent(blocks[3], low ^ high)
    )


def block_places(count, rows):
    codes = jnp.repeat(jnp.asarray(block_codes(count), jnp.int32), rows)
    offsets = jnp.tile(jnp.arange(rows, dtype=jnp.int32), count)
    return (codes ^ lax.axis_index("dp")) * rows + offsets


def one_hot_rows(places, count):
    return (jnp.arange(count, dtype=jnp.int32)[:, None] == places[None, :]).astype(jnp.bfloat16)


def chosen(rows, order):
    return jnp.dot(rows, order, preferred_element_type=jnp.float32).astype(jnp.bfloat16)


def document_rows(lengths, row_ids):
    ends = jnp.cumsum(lengths)
    starts = ends - lengths
    segments = jnp.sum((row_ids[:, None] >= ends[None, :]).astype(jnp.int32), axis=1)
    used_rows = ends[-1]
    matches = segments[:, None] == jnp.arange(lengths.shape[0], dtype=jnp.int32)[None, :]
    anchor = jnp.sum(jnp.where(matches, starts[None, :], 0), axis=1)
    anchor = anchor + jnp.where(segments == lengths.shape[0], used_rows, 0)
    validity = (row_ids < used_rows).astype(jnp.float32)
    return (segments, row_ids - anchor, validity)


def schulz(gram, rows):
    scale = 1.0 / (jnp.sqrt(jnp.trace(gram.astype(jnp.float32))) + 1e-07)
    gram = gram.astype(jnp.float32) * scale * scale
    current = (rows.astype(jnp.float32) * scale).astype(jnp.bfloat16)
    for repeat in range(ORTHO_STEPS):
        narrow = gram.astype(jnp.bfloat16)
        mixing = (
            SCHULZ_CUBIC * gram
            + SCHULZ_QUINTIC * jnp.dot(narrow, narrow, preferred_element_type=jnp.float32)
        ).astype(jnp.bfloat16)
        current = (
            SCHULZ_LINEAR * current.astype(jnp.float32)
            + jnp.dot(current, mixing, preferred_element_type=jnp.float32)
        ).astype(jnp.bfloat16)
        once = SCHULZ_LINEAR * gram + jnp.dot(narrow, mixing, preferred_element_type=jnp.float32)
        gram = SCHULZ_LINEAR * once + jnp.dot(
            once.astype(jnp.bfloat16), mixing, preferred_element_type=jnp.float32
        )
    return current


def spread(term, own_rows):
    return term[:own_rows] + swap(term[own_rows:].astype(jnp.bfloat16)).astype(jnp.float32)


def join(values):
    return jnp.concatenate([values, swap(values)], axis=0)


def on_device(
    layer_input,
    upstream_grad,
    doc_lengths,
    qkv_weight,
    out_weight,
    gate_weight,
    up_weight,
    down_weight,
    qkv_momentum,
    out_momentum,
    gate_momentum,
    up_momentum,
    down_momentum,
    norm_gains,
    norm_biases,
    adam_first,
    adam_second,
):
    part_rows, model_width = layer_input.shape
    core = lax.axis_index("mp")
    dp_count = lax.axis_size("dp")
    dp_index = lax.axis_index("dp")
    head_rows = out_weight.shape[0]
    hidden_rows = gate_weight.shape[0]
    local_width = head_rows * dp_count
    local_heads = local_width // HD
    local_hidden = hidden_rows * dp_count

    tokens = join(layer_input)
    norm_params = jnp.concatenate([norm_gains, norm_biases])
    norm_width = norm_params.shape[1]
    norm_pad = jnp.pad(norm_params.reshape(1, -1), ((0, 15), (0, model_width - 4 * norm_width)))
    attn_blocks = gather_blocks(
        jnp.concatenate(
            [qkv_weight.reshape(-1, model_width), out_weight, norm_pad], axis=0
        ).astype(jnp.bfloat16)
    )
    gate_up_blocks = gather_blocks(
        jnp.concatenate([gate_weight, up_weight], axis=0).astype(jnp.bfloat16)
    )
    down_blocks = gather_blocks(down_weight.astype(jnp.bfloat16))

    pair_rows = 2 * head_rows
    places = block_places(dp_count, pair_rows)
    kind, place = places % pair_rows // head_rows, places // pair_rows * head_rows
    head_order = one_hot_rows(
        kind * local_width + place + places % head_rows, 2 * local_width
    )
    query_key_weight = chosen(
        head_order, attn_blocks[:, :pair_rows].reshape(2 * local_width, model_width)
    )
    value_out_weight = chosen(
        head_order, attn_blocks[:, pair_rows : 2 * pair_rows].reshape(2 * local_width, model_width)
    )
    qkv_flat = jnp.concatenate([query_key_weight, value_out_weight[:local_width]], axis=0)
    out_full = value_out_weight[local_width:]
    norm_blocks = attn_blocks[:, 2 * pair_rows, : 4 * norm_width].reshape(dp_count, 4, norm_width)
    norm_order = one_hot_rows(block_places(dp_count, 1), dp_count)
    norm_wide = jnp.einsum(
        "ij,jpw->piw", norm_order, norm_blocks, preferred_element_type=jnp.float32
    ).reshape(4, model_width)
    gains_wide, biases_wide = norm_wide[:2], norm_wide[2:]
    gate_full = gate_up_blocks[:, :hidden_rows].reshape(local_hidden, model_width)
    up_full = gate_up_blocks[:, hidden_rows:].reshape(local_hidden, model_width)
    down_full = down_blocks.reshape(local_hidden, model_width)

    own_ids = core * part_rows + jnp.arange(part_rows, dtype=jnp.int32)
    other_ids = (1 - core) * part_rows + jnp.arange(part_rows, dtype=jnp.int32)
    segments, positions, validity = document_rows(
        doc_lengths[0], jnp.concatenate([own_ids, other_ids])
    )
    total_rows = 2 * part_rows
    cosine_table, sine_table = rotary_tables(positions)
    projected = times_transposed(tokens, qkv_flat)
    columns_split = projected.reshape(total_rows, 3, local_heads, HD)
    queries = rotate(columns_split[:, 0], cosine_table, sine_table).astype(jnp.bfloat16)
    key_vectors = rotate(columns_split[:, 1], cosine_table, sine_table).astype(jnp.bfloat16)
    value_vectors = columns_split[:, 2].astype(jnp.bfloat16)
    attended = attend(queries, key_vectors, value_vectors, segments)
    mixed_heads = attended.reshape(total_rows, local_width).astype(jnp.bfloat16)
    branch = spread(jnp.dot(mixed_heads, out_full, preferred_element_type=jnp.float32), part_rows)
    first_out, normed_one, inverse_one = layer_norm(
        layer_input.astype(jnp.float32) + branch, gains_wide[0], biases_wide[0]
    )
    inner_tokens = join(first_out.astype(jnp.bfloat16))
    gate_pre = times_transposed(inner_tokens, gate_full)
    up_pre = times_transposed(inner_tokens, up_full)
    gate_sigmoid = jax.nn.sigmoid(gate_pre)
    silu_value = gate_pre * gate_sigmoid
    activated = (silu_value * up_pre).astype(jnp.bfloat16)
    feed = spread(jnp.dot(activated, down_full, preferred_element_type=jnp.float32), part_rows)
    final_out, normed_two, inverse_two = layer_norm(first_out + feed, gains_wide[1], biases_wide[1])
    mixed = final_out.astype(jnp.bfloat16)

    cotangent = upstream_grad.astype(jnp.float32) * validity[:part_rows, None]
    grad_second, gain_two_grad, bias_two_grad = norm_back(
        cotangent, normed_two, inverse_two, gains_wide[1]
    )
    feed_grad = join(grad_second.astype(jnp.bfloat16))
    down_weight_grad = transposed_times(activated, feed_grad).astype(jnp.bfloat16)
    down_sum = scatter_blocks(down_weight_grad.reshape(dp_count, hidden_rows, model_width))
    hidden_grad = times_transposed(feed_grad, down_full)
    up_grad_rows = (hidden_grad * silu_value).astype(jnp.bfloat16)
    gate_grad_rows = (
        hidden_grad * up_pre * gate_sigmoid * (1.0 + gate_pre * (1.0 - gate_sigmoid))
    ).astype(jnp.bfloat16)
    inner_grad = jnp.dot(gate_grad_rows, gate_full, preferred_element_type=jnp.float32) + jnp.dot(
        up_grad_rows, up_full, preferred_element_type=jnp.float32
    )
    gate_weight_grad = transposed_times(gate_grad_rows, inner_tokens).astype(jnp.bfloat16)
    up_weight_grad = transposed_times(up_grad_rows, inner_tokens).astype(jnp.bfloat16)
    gate_up_sum = scatter_blocks(
        jnp.concatenate(
            [
                gate_weight_grad.reshape(dp_count, hidden_rows, model_width),
                up_weight_grad.reshape(dp_count, hidden_rows, model_width),
            ],
            axis=1,
        )
    )
    first_grad_total = grad_second + spread(inner_grad, part_rows)
    grad_first, gain_one_grad, bias_one_grad = norm_back(
        first_grad_total, normed_one, inverse_one, gains_wide[0]
    )
    branch_grad = join(grad_first.astype(jnp.bfloat16))
    padded_rows = head_rows + -head_rows % 16
    single_order = jnp.pad(
        one_hot_rows(block_places(dp_count, head_rows), local_width).reshape(
            local_width, dp_count, head_rows
        ),
        ((0, 0), (0, 0), (0, padded_rows - head_rows)),
    ).reshape(local_width, dp_count * padded_rows)
    out_weight_grad = transposed_times(chosen(mixed_heads, single_order), branch_grad)
    out_sum = scatter_blocks(
        out_weight_grad.astype(jnp.bfloat16).reshape(dp_count, padded_rows, model_width)
    )[:head_rows]
    heads_grad = (
        times_transposed(branch_grad, out_full)
        .astype(jnp.bfloat16)
        .reshape(total_rows, local_heads, HD)
    )
    query_grad, key_grad, value_grad = attend_back(
        queries, key_vectors, value_vectors, segments, heads_grad
    )
    query_key_grad = jnp.concatenate(
        [
            unrotate(query_grad, cosine_table, sine_table).reshape(total_rows, local_width),
            unrotate(key_grad, cosine_table, sine_table).reshape(total_rows, local_width),
        ],
        axis=1,
    ).astype(jnp.bfloat16)
    value_grad = value_grad.reshape(total_rows, local_width).astype(jnp.bfloat16)
    qkv_grad = jnp.concatenate([query_key_grad, value_grad], axis=1)
    qkv_weight_grad = jnp.concatenate(
        [
            transposed_times(chosen(query_key_grad, head_order), tokens)
            .astype(jnp.bfloat16)
            .reshape(dp_count, pair_rows, model_width),
            transposed_times(chosen(value_grad, single_order), tokens)
            .astype(jnp.bfloat16)
            .reshape(dp_count, padded_rows, model_width),
        ],
        axis=1,
    )
    qkv_sum = scatter_blocks(qkv_weight_grad)[: 3 * head_rows].reshape(qkv_weight.shape)
    input_grad = grad_first + spread(
        jnp.dot(qkv_grad, qkv_flat, preferred_element_type=jnp.float32), part_rows
    )

    norm_totals = jnp.stack([gain_one_grad, gain_two_grad, bias_one_grad, bias_two_grad])
    norm_totals = norm_totals + swap(norm_totals)
    for mask in [1 << k for k in range(dp_count.bit_length() - 1)]:
        norm_totals = norm_totals + flip(norm_totals, mask)

    momenta = (qkv_momentum, out_momentum, gate_momentum, up_momentum, down_momentum)
    summed = (qkv_sum, out_sum, gate_up_sum[:hidden_rows], gate_up_sum[hidden_rows:], down_sum)
    carried = [MOMENTUM_KEEP * moment + gradient for moment, gradient in zip(momenta, summed)]
    qkv_rows, out_rows, gate_rows, up_rows, down_rows = [
        value.astype(jnp.bfloat16).reshape(-1, model_width) for value in carried
    ]

    first_core = core == 0
    lent = swap(jnp.stack([jnp.where(first_core, down_rows, gate_rows), up_rows]))
    pair_one = jnp.concatenate([jnp.where(first_core, gate_rows, down_rows), lent[0]])
    pair_up = jnp.concatenate([up_rows, lent[1]])
    block = model_width // dp_count
    half_width = model_width // 2
    order = one_hot_rows(block_places(dp_count, block), model_width)
    half_up = jnp.where(first_core, pair_up[:, :half_width], pair_up[:, half_width:])
    gram_rows = jnp.concatenate(
        [
            transposed_times(chosen(pair_one, order), pair_one),
            transposed_times(chosen(pair_up, order), half_up),
        ],
        axis=1,
    ).astype(jnp.bfloat16)
    gram_sum = scatter_blocks(gram_rows.reshape(dp_count, block, model_width + half_width))
    gram_rows = chosen(
        order,
        gather_blocks(gram_sum.astype(jnp.bfloat16)).reshape(model_width, model_width + half_width),
    )
    gram_one = gram_rows[:, :model_width]
    gram_up = gram_rows[:, model_width:]
    gram_up = jnp.concatenate([gram_up, swap(gram_up)], axis=1)
    done_one = schulz(gram_one, pair_one)

    out_padded = jnp.pad(out_rows, ((0, padded_rows - head_rows), (0, 0)))
    out_whole = join(gather_blocks(out_padded).reshape(dp_count * padded_rows, model_width))
    done_out = schulz(
        transposed_times(out_whole, out_whole),
        out_padded,
    )[:head_rows]

    qkv_whole = gather_blocks(jnp.pad(qkv_rows, ((0, -3 * head_rows % 16), (0, 0))))
    qkv_whole = qkv_whole.reshape(-1, model_width)
    gram_qkv = transposed_times(qkv_whole, qkv_whole)
    gram_qkv = gram_qkv + swap(gram_qkv.astype(jnp.bfloat16)).astype(jnp.float32)
    qkv_padded = jnp.pad(qkv_rows, ((0, hidden_rows - 3 * head_rows), (0, 0)))
    pair_two = jnp.where(first_core, pair_up, join(qkv_padded))
    done_two = schulz(jnp.where(first_core, gram_up.astype(jnp.float32), gram_qkv), pair_two)
    returned = swap(jnp.stack([done_one[hidden_rows:], done_two[hidden_rows:]]))
    pieces = (
        jnp.where(first_core, returned[1], done_two[:hidden_rows])[: 3 * head_rows].reshape(
            qkv_weight.shape
        ),
        done_out,
        jnp.where(first_core, done_one[:hidden_rows], returned[0]),
        jnp.where(first_core, done_two[:hidden_rows], returned[1]),
        jnp.where(first_core, returned[0], done_one[:hidden_rows]),
    )
    weights = (qkv_weight, out_weight, gate_weight, up_weight, down_weight)
    row_totals = (3 * D, D, FF, FF, FF)
    updated = [
        weight * (1.0 - ORTHO_RATE * WEIGHT_DECAY)
        - ORTHO_RATE * 0.2 * math.sqrt(row_total) * piece.astype(jnp.float32)
        for weight, piece, row_total in zip(weights, pieces, row_totals)
    ]
    width_part = adam_first.shape[1]
    norm_grad = lax.dynamic_slice_in_dim(norm_totals, dp_index * width_part, width_part, 1)
    norm_now = jnp.concatenate([norm_gains, norm_biases], axis=0)
    norm_first = BETA_FIRST * adam_first + (1.0 - BETA_FIRST) * norm_grad
    norm_second = BETA_SECOND * adam_second + (1.0 - BETA_SECOND) * norm_grad * norm_grad
    first_hat = norm_first / (1.0 - BETA_FIRST**STEP_COUNT)
    second_hat = norm_second / (1.0 - BETA_SECOND**STEP_COUNT)
    norm_updated = norm_now - ADAM_RATE * first_hat / (jnp.sqrt(second_hat) + ADAM_EPSILON)
    return (
        mixed,
        input_grad,
        updated[0],
        updated[1],
        updated[2],
        updated[3],
        updated[4],
        carried[0],
        carried[1],
        carried[2],
        carried[3],
        carried[4],
        norm_updated,
        norm_first,
        norm_second,
    )


def solution(mesh):
    return jax.shard_map(
        on_device,
        mesh=mesh,
        in_specs=(
            P(("dp", "mp"), None),
            P(("dp", "mp"), None),
            P("dp", None),
            P(None, ("mp", "dp"), None),
            P(("mp", "dp"), None),
            P(("mp", "dp"), None),
            P(("mp", "dp"), None),
            P(("mp", "dp"), None),
            P(None, ("mp", "dp"), None),
            P(("mp", "dp"), None),
            P(("mp", "dp"), None),
            P(("mp", "dp"), None),
            P(("mp", "dp"), None),
            P(None, "dp"),
            P(None, "dp"),
            P(None, "dp"),
            P(None, "dp"),
        ),
        out_specs=(
            P(("dp", "mp"), None),
            P(("dp", "mp"), None),
            P(None, ("mp", "dp"), None),
            P(("mp", "dp"), None),
            P(("mp", "dp"), None),
            P(("mp", "dp"), None),
            P(("mp", "dp"), None),
            P(None, ("mp", "dp"), None),
            P(("mp", "dp"), None),
            P(("mp", "dp"), None),
            P(("mp", "dp"), None),
            P(("mp", "dp"), None),
            P(None, "dp"),
            P(None, "dp"),
            P(None, "dp"),
        ),
        check_vma=False,
    )
```
